512 devices in a mesh: section: 16 (over z_hi, x), dp: 32 (over z_lo, y, core).
Axes of the slice: x: 4, y: 4, z: 16 (z_hi: 4, z_lo: 4; z = z_hi * 4 + z_lo), core: 2. Of those that a mesh axis runs over, the one named last changes fastest.
Arguments:
- boundary_in: bfloat16 [8192, 640], P('dp'), may hold values from -6 to 6
- weights: bfloat16 [16, 2560, 640], P('section', 'dp'), may hold values from -0.125 to 0.125
- gains: float32 [16, 2560], P('section'), may hold values from 0.5 to 2
- cotangent: bfloat16 [8192, 640], P('dp'), may hold values from -6 to 6
Outputs:
- weight_grad: float32 [16, 2560, 640], P('section', 'dp')
- section_grad: bfloat16 [16, 8192, 640], P('section', 'dp')
The draws below stay inside these ranges and needn't reach their ends.
All inputs are finite; a program needn't handle non-finite values.
Results may differ from the reference program's by a relative error of at most 0.035.
Values may be sent and summed in bfloat16 or wider, within the bound.
A program may use at most 64 MiB of HBM per device.

```python
import math
import jax
import jax.numpy as jnp
from jax import lax

H = 2560
C = 640
TOK_DEV = 256
SECTIONS = 16
TOKENS = 8192
N_DP = 32


def levels(key, shape, shards, least, largest):
    gain = 1.0
    for position, shards_of in shards:
        steps = jax.random.uniform(jax.random.fold_in(jax.random.fold_in(key, 6), position), (shards_of,), jnp.float32, least / len(shards), largest / len(shards))
        gain = gain * jnp.repeat(jnp.exp(steps), shape[position] // shards_of).reshape((-1,) + (1,) * (len(shape) - 1 - position))
    return gain


def centred(stream_key, extent, width, limit, split=(), dtype=jnp.bfloat16):
    level = levels(stream_key, extent, split, -0.22, 0.18) if split else 1.0
    entries = jax.random.normal(stream_key, extent, jnp.float32) * width * level
    return jnp.minimum(jnp.maximum(entries, -limit), limit).astype(dtype)


def setup_inputs(seed: int = 0) -> dict:
    streams_of = jax.random.split(jax.random.key(seed), 5)
    boundary_in = centred(streams_of[0], (TOKENS, C), 1.0, 6.0, ((0, 32),))
    weights = centred(streams_of[1], (SECTIONS, H, C), H ** -0.5, 0.125, ((0, 16), (1, 32)))
    gains = jnp.clip(0.5 + 1.5 * jax.random.uniform(streams_of[2], (SECTIONS, H), jnp.float32) ** levels(streams_of[2], (SECTIONS, H), ((0, 16),), -0.2, 0.2), 0.5, 2.0)
    cotangent = centred(streams_of[3], (TOKENS, C), 1.0, 6.0, ((0, 32),))
    return {"boundary_in": boundary_in, "weights": weights, "gains": gains, "cotangent": cotangent}


def activate(pre_norm, gain_row):
    inv_rms = lax.rsqrt(lax.optimization_barrier(jnp.mean(pre_norm * pre_norm, axis=1, keepdims=True)) + 1e-05)
    normed = pre_norm * inv_rms * gain_row
    return (inv_rms, normed, jax.nn.silu(normed).astype(jnp.bfloat16))

def replica_sums(left, right):
    left_parts = left.astype(jnp.float32).reshape(N_DP, TOK_DEV, left.shape[1])
    right_parts = right.astype(jnp.float32).reshape(N_DP, TOK_DEV, right.shape[1])
    return jnp.einsum('krh,krc->khc', left_parts, right_parts)

def reference(boundary_in, weights, gains, cotangent):
    inputs = []
    current = boundary_in
    for section in range(SECTIONS):
        inputs.append(current)
        pre_norm = jnp.dot(current, weights[section].T, preferred_element_type=jnp.float32)
        inv_rms, normed, activated = activate(pre_norm, gains[section])
        current = (current.astype(jnp.float32) + jnp.dot(activated, weights[section], preferred_element_type=jnp.float32)).astype(jnp.bfloat16)
    grad_out = cotangent
    section_grads = []
    weight_grads = []
    for section in reversed(range(SECTIONS)):
        weight = weights[section]
        gain_row = gains[section]
        block_input = inputs[section]
        pre_norm = jnp.dot(block_input, weight.T, preferred_element_type=jnp.float32)
        inv_rms, normed, activated = activate(pre_norm, gain_row)
        grad_act = jnp.dot(grad_out, weight.T, preferred_element_type=jnp.float32)
        sigmoid_h = jax.nn.sigmoid(normed)
        grad_normed = grad_act * sigmoid_h * (1.0 + normed * (1.0 - sigmoid_h)) * gain_row
        grad_pre = (inv_rms * (grad_normed - pre_norm * inv_rms * inv_rms * lax.optimization_barrier(jnp.mean(grad_normed * pre_norm, axis=1, keepdims=True)))).astype(jnp.bfloat16)
        grad_in = (grad_out.astype(jnp.float32) + jnp.dot(grad_pre, weight, preferred_element_type=jnp.float32)).astype(jnp.bfloat16)
        partial_value = (replica_sums(grad_pre, block_input) + replica_sums(activated, grad_out)).astype(jnp.bfloat16)
        partial_value = lax.optimization_barrier(partial_value).astype(jnp.float32)
        weight_grads.append(lax.optimization_barrier(jnp.sum(partial_value, axis=0)) / math.sqrt(TOKENS))
        section_grads.append(grad_in)
        grad_out = grad_in
    weight_grads = weight_grads[::-1]
    section_grads = section_grads[::-1]
    return (jnp.stack(weight_grads), jnp.stack(section_grads))
```

```python
import math

import jax
import jax.numpy as jnp
from jax import lax
from jax.experimental import pallas as pl
from jax.experimental.pallas import tpu as pltpu
from jax.sharding import PartitionSpec as P

MESH = pl.DeviceIdType.MESH
BF, F32 = jnp.bfloat16, jnp.float32
C, H, T = 640, 2560, 64
ROWS, LANES = 80, 128
PLANS = 5
BLOCKS = 128


def bits_of(s, zl, y, c):
    xu, yu = lax.div(s, 2), lax.div(y, 2)
    xv, yv = lax.rem(lax.rem(s, 2) + xu, 2), lax.rem(lax.rem(y, 2) + yu, 2)
    return [xu, yu, lax.rem(zl, 2), xv, yv], lax.div(zl, 2), c


def place(plan, s, zl, y, c):
    dims, zb, core = bits_of(s, zl, y, c)
    at = zb + 64 * core
    for i in range(5):
        at = at + dims[(plan + i) % 5] * (2 << i)
    return at


def kernel(b_ref, w_ref, gain_ref, cot_ref, wg_ref, sg_ref,
           g, r, w, gains, xh, dn, da, cg, c_in, c_out, g_in, g_out, x_send,
           ag_s, ag_r, rs_s, rs_r, gn_s, gn_r, hop_s, hop_r, sg_s, sg_r):
    sec, dp = lax.axis_index("section"), lax.axis_index("dp")
    j, x = lax.div(sec, 4), lax.rem(sec, 4)
    zl, y, c = lax.div(dp, 8), lax.rem(lax.div(dp, 2), 4), lax.rem(dp, 2)

    def device(j, x, zl, y, c):
        return (j * 4 + x, zl * 8 + y * 2 + c)

    def flip(v):
        return v + 1 - 2 * lax.rem(v, 2)

    partner = [
        device(j, 3 - x, zl, y, c),
        device(j, x, zl, 3 - y, c),
        device(j, x, flip(zl), y, c),
        device(j, flip(x), zl, y, c),
        device(j, x, zl, flip(y), c),
    ]
    zb_partner = device(j, x, lax.rem(zl + 2, 4), y, c)
    core_partner = device(j, x, zl, y, 1 - c)
    ahead = device(lax.rem(j + 1, 4), x, zl, y, c)
    behind = device(lax.rem(j + 3, 4), x, zl, y, c)
    beside = [device(j, lax.rem(x + i, 4), zl, y, c) for i in (1, 2, 3)]

    barrier = pltpu.get_barrier_semaphore()
    peers = partner + [zb_partner, core_partner, ahead, behind, beside[1]]
    for peer in peers:
        pl.semaphore_signal(barrier, inc=1, device_id=peer, device_id_type=MESH)

    mine = [place(p, x, zl, y, c) for p in range(PLANS)]
    for p in range(PLANS):
        g[p, mine[p]] = w_ref[0, :, p * LANES:(p + 1) * LANES]
    gains[x] = gain_ref[...]
    pl.semaphore_wait(barrier, len(peers))

    def remote(src, dst, send, recv, to):
        return pltpu.make_async_remote_copy(
            src_ref=src, dst_ref=dst, send_sem=send, recv_sem=recv, device_id=to, device_id_type=MESH
        )

    def span(p, step):
        n = 1 << step
        return pl.ds(lax.div(mine[p], n) * n, n)

    def target(p, step):
        if step == 0:
            return zb_partner
        if step == 6:
            return core_partner
        return partner[(p + step - 1) % 5]

    gain_copies = [
        remote(gains.at[x], gains.at[x], gn_s.at[i], gn_r.at[i], beside[i]) for i in range(3)
    ]
    started = []
    for step in range(7):
        copies = []
        for p in range(PLANS):
            part = g.at[p, span(p, step)]
            copies.append(remote(part, part, ag_s.at[step, p], ag_r.at[step, p], target(p, step)))
            copies[-1].start()
        if step == 0:
            for copy in gain_copies:
                copy.start()
        for copy in copies:
            copy.wait_recv()
        started += copies
    for copy in gain_copies:
        copy.wait()
    for copy in started:
        copy.wait_send()

    def repack(i, carry):
        s, k = lax.div(i, 32), lax.rem(i, 32)
        z_, y_, c_ = lax.div(k, 8), lax.rem(lax.div(k, 2), 4), lax.rem(k, 2)
        for p in range(PLANS):
            w[s, pl.ds(pl.multiple_of(k * ROWS, 16), ROWS), p * LANES:(p + 1) * LANES] = g[p, place(p, s, z_, y_, c_)]
        return carry

    lax.fori_loop(0, 4 * 32, repack, 0)

    first = hop = None
    fwd = remote(c_out, c_in, hop_s.at[0], hop_r.at[0], ahead)
    bwd = remote(g_out, g_in, hop_s.at[1], hop_r.at[1], behind)

    @pl.when(j == 0)
    def _():
        c_out[...] = b_ref[pl.ds(pl.multiple_of(x * T, T), T), :]

    @pl.when(j > 0)
    def _():
        fwd.wait_recv()
        c_out[...] = c_in[...]

    def forward(s, carry):
        block = c_out[...]
        cg[s, :T, :] = block
        pre = lax.dot_general(block, w[s], (((1,), (1,)), ((), ())), preferred_element_type=F32)
        inv = lax.rsqrt(jnp.mean(pre * pre, axis=1, keepdims=True) + 1e-05)
        hat = pre * inv
        gain = gains[s]
        normed = hat * gain
        sig = 1.0 / (1.0 + jnp.exp(-normed))
        act = (normed * sig).astype(BF)
        xh[s] = hat
        dn[s] = sig * (1.0 + normed * (1.0 - sig)) * gain * inv
        da[s, T:, :] = act
        c_out[...] = (block.astype(F32) + jnp.dot(act, w[s], preferred_element_type=F32)).astype(BF)
        return carry

    lax.fori_loop(0, 4, forward, 0)

    @pl.when(j < 3)
    def _():
        fwd.start()

    @pl.when(j == 3)
    def _():
        g_out[...] = cot_ref[pl.ds(pl.multiple_of(x * T, T), T), :]

    @pl.when(j < 3)
    def _():
        bwd.wait_recv()
        g_out[...] = g_in[...]

    def backward(i, carry):
        s = 3 - i
        grad = g_out[...]
        cg[s, T:, :] = grad
        e = lax.dot_general(grad, w[s], (((1,), (1,)), ((), ())), preferred_element_type=F32) * dn[s]
        hat = xh[s]
        dpre = (e - hat * jnp.mean(e * hat, axis=1, keepdims=True)).astype(BF)
        da[s, :T, :] = dpre
        grad_in = (grad.astype(F32) + jnp.dot(dpre, w[s], preferred_element_type=F32)).astype(BF)
        g_out[...] = grad_in
        x_send[s] = grad_in
        return carry

    lax.fori_loop(0, 4, backward, 0)

    @pl.when(j > 0)
    def _():
        bwd.start()

    rows = pl.ds(pl.multiple_of(x * T, T), T)
    sg_ref[0, rows, :] = x_send[x]
    sg_copies = [
        remote(x_send.at[lax.rem(x + i, 4)], sg_ref.at[0, rows], sg_s.at[i - 1], sg_r.at[i - 1], beside[i - 1])
        for i in (1, 2, 3)
    ]
    for copy in sg_copies:
        copy.start()

    def outer(i, carry):
        s, z_ = lax.div(i, 4), lax.rem(i, 4)
        left = da[s, :, pl.ds(pl.multiple_of(z_ * 640, 128), 640)]
        grad = lax.dot_general(left, cg[s], (((0,), (0,)), ((), ())), preferred_element_type=F32).astype(BF)
        for t in range(8):
            for p in range(PLANS):
                g[p, place(p, s, z_, t // 2, t % 2)] = grad[t * ROWS:(t + 1) * ROWS, p * LANES:(p + 1) * LANES]
        return carry

    lax.fori_loop(0, 16, outer, 0)

    started = []
    for step in (6, 5, 4, 3, 2, 1, 0):
        n = 1 << step
        copies = []
        for p in range(PLANS):
            keep = lax.div(mine[p], n) * n
            away = keep + n - 2 * n * lax.rem(lax.div(mine[p], n), 2)
            copies.append(remote(g.at[p, pl.ds(away, n)], r.at[p, pl.ds(n - 1, n)], rs_s.at[step, p], rs_r.at[step, p], target(p, step)))
            copies[-1].start()
        started += copies
        for p in range(PLANS):
            keep = lax.div(mine[p], n) * n
            copies[p].wait_recv()

            def add(i, carry, p=p, keep=keep, n=n):
                g[p, keep + i] = g[p, keep + i] + r[p, n - 1 + i]
                return carry

            lax.fori_loop(0, n, add, 0, unroll=min(n, 8))

    for p in range(PLANS):
        wg_ref[0, :, p * LANES:(p + 1) * LANES] = g[p, mine[p]].astype(F32) * (1.0 / math.sqrt(8192))
    for copy in started:
        copy.wait_send()
    for copy in sg_copies:
        copy.wait()

    @pl.when(j < 3)
    def _():
        fwd.wait_send()

    @pl.when(j > 0)
    def _():
        bwd.wait_send()


def shards(boundary_in, weights, gains, cotangent):
    vmem = pl.BlockSpec(memory_space=pltpu.VMEM)
    dma = pltpu.SemaphoreType.DMA
    return pl.pallas_call(
        kernel,
        out_shape=(
            jax.ShapeDtypeStruct((1, ROWS, C), F32),
            jax.ShapeDtypeStruct((1, 4 * T, C), BF),
        ),
        in_specs=[vmem] * 4,
        out_specs=(vmem, vmem),
        scratch_shapes=[
            pltpu.VMEM((PLANS, BLOCKS, ROWS, LANES), BF),
            pltpu.VMEM((PLANS, BLOCKS, ROWS, LANES), BF),
            pltpu.VMEM((4, H, C), BF),
            pltpu.VMEM((4, 1, H), F32),
            pltpu.VMEM((4, T, H), F32),
            pltpu.VMEM((4, T, H), F32),
            pltpu.VMEM((4, 2 * T, H), BF),
            pltpu.VMEM((4, 2 * T, C), BF),
            pltpu.VMEM((T, C), BF),
            pltpu.VMEM((T, C), BF),
            pltpu.VMEM((T, C), BF),
            pltpu.VMEM((T, C), BF),
            pltpu.VMEM((4, T, C), BF),
            dma((7, PLANS)),
            dma((7, PLANS)),
            dma((7, PLANS)),
            dma((7, PLANS)),
            dma((3,)),
            dma((3,)),
            dma((2,)),
            dma((2,)),
            dma((3,)),
            dma((3,)),
        ],
        compiler_params=pltpu.CompilerParams(
            collective_id=0, has_side_effects=True, vmem_limit_bytes=60 << 20
        ),
    )(boundary_in, weights, gains, cotangent)


def solution(mesh):
    return jax.shard_map(
        shards,
        mesh=mesh,
        in_specs=(P("dp", None), P("section", "dp", None), P("section", None), P("dp", None)),
        out_specs=(P("section", "dp", None), P("section", "dp", None)),
        check_vma=False,
    )
```

```python
import math

import jax
import jax.numpy as jnp
from jax import lax
from jax.experimental import pallas as pl
from jax.experimental.pallas import tpu as pltpu
from jax.sharding import PartitionSpec as P

MESH = pl.DeviceIdType.MESH
BF, F32 = jnp.bfloat16, jnp.float32
C, H, T = 640, 2560, 64
ROWS, LANES = 80, 128
PLANS = 5
BLOCKS = 128
HALF = H // 2
STREAMS = (slice(0, 48), slice(48, 80))


def bits_of(s, zl, y, c):
    xu, yu = lax.div(s, 2), lax.div(y, 2)
    xv, yv = lax.rem(lax.rem(s, 2) + xu, 2), lax.rem(lax.rem(y, 2) + yu, 2)
    return [xu, yu, lax.rem(zl, 2), xv, yv], lax.div(zl, 2), c


def place(plan, s, zl, y, c):
    dims, zb, core = bits_of(s, zl, y, c)
    at = zb + 64 * core
    for i in range(5):
        at = at + dims[(plan + i) % 5] * (2 << i)
    return at


def kernel(b_ref, w_ref, gain_ref, cot_ref, wg_ref, sg_ref,
           g, r, w, wt, gains, xh, dn, acts, acts_o, dpre, dpre_o, cs, cs_o, gs, gs_o,
           c_in, c_out, g_in, g_out, x_send,
           ag_s, ag_r, co_s, co_r, rs_s, rs_r, gn_s, gn_r, hop_s, hop_r, sg_s, sg_r, ex_s, ex_r):
    sec, dp = lax.axis_index("section"), lax.axis_index("dp")
    j, x = lax.div(sec, 4), lax.rem(sec, 4)
    zl, y, c = lax.div(dp, 8), lax.rem(lax.div(dp, 2), 4), lax.rem(dp, 2)

    def device(j, x, zl, y, c):
        return (j * 4 + x, zl * 8 + y * 2 + c)

    def flip(v):
        return v + 1 - 2 * lax.rem(v, 2)

    partner = [
        device(j, 3 - x, zl, y, c),
        device(j, x, zl, 3 - y, c),
        device(j, x, flip(zl), y, c),
        device(j, flip(x), zl, y, c),
        device(j, x, zl, flip(y), c),
    ]
    zb_partner = device(j, x, lax.rem(zl + 2, 4), y, c)
    core_partner = device(j, x, zl, y, 1 - c)
    ahead = device(lax.rem(j + 1, 4), x, zl, y, c)
    behind = device(lax.rem(j + 3, 4), x, zl, y, c)
    beside = [device(j, lax.rem(x + i, 4), zl, y, c) for i in (1, 2, 3)]

    barrier = pltpu.get_barrier_semaphore()
    peers = partner + [zb_partner, core_partner, ahead, behind, beside[1]]
    for peer in peers:
        pl.semaphore_signal(barrier, inc=1, device_id=peer, device_id_type=MESH)

    mine = [place(p, x, zl, y, c) for p in range(PLANS)]
    for p in range(PLANS):
        g[p, mine[p]] = w_ref[0, :, p * LANES:(p + 1) * LANES]
    gains[x] = jnp.concatenate(
        [gain_ref[:, (2 * i + h) * ROWS:(2 * i + h + 1) * ROWS] for h in (0, 1) for i in range(16)], axis=1
    )
    pl.semaphore_wait(barrier, len(peers))

    def remote(src, dst, send, recv, to):
        return pltpu.make_async_remote_copy(
            src_ref=src, dst_ref=dst, send_sem=send, recv_sem=recv, device_id=to, device_id_type=MESH
        )

    def target(p, step):
        return zb_partner if step == 0 else partner[(p + step - 1) % 5]

    def held(p, step):
        n = 1 << step
        return lax.div(mine[p], n) * n

    def other(p, step):
        n = 1 << step
        return held(p, step) + n - 2 * n * lax.rem(lax.div(mine[p], n), 2)

    def gather(p, step, h):
        part = g.at[p, pl.ds(held(p, step), 1 << step), STREAMS[h]]
        return remote(part, part, ag_s.at[step, p, h], ag_r.at[step, p, h], target(p, step))

    def across(p, late, h):
        part = g.at[p, pl.ds(other(p, 5) if late else held(p, 5), 32), STREAMS[h]]
        return remote(part, part, co_s.at[late, p, h], co_r.at[late, p, h], core_partner)

    gain_copies = [
        remote(gains.at[x], gains.at[x], gn_s.at[i], gn_r.at[i], beside[i]) for i in range(3)
    ]
    every = [(h, p) for h in range(2) for p in range(PLANS)]
    for h, p in every:
        gather(p, 0, h).start()
    for copy in gain_copies:
        copy.start()
    for step in range(1, 6):
        for h, p in every:
            gather(p, step - 1, h).wait_recv()
            gather(p, step, h).start()
    for h, p in every:
        across(p, 0, h).start()
    for h, p in every:
        gather(p, 5, h).wait_recv()
        across(p, 1, h).start()
    for copy in gain_copies:
        copy.wait()
    for h, p in every:
        across(p, 0, h).wait_recv()
        across(p, 1, h).wait_recv()

    def repack(i, carry):
        s, k = lax.div(i, 32), lax.rem(i, 32)
        c_, z_, y_ = lax.div(k, 16), lax.rem(lax.div(k, 4), 4), lax.rem(k, 4)
        for p in range(PLANS):
            w[s, pl.ds(pl.multiple_of(k * ROWS, 16), ROWS), p * LANES:(p + 1) * LANES] = g[p, place(p, s, z_, y_, c_)]
        return carry

    lax.fori_loop(0, 4 * 32, repack, 0)

    def transpose(i, carry):
        s, k = lax.div(i, 10), lax.rem(i, 10)
        at = pl.ds(pl.multiple_of(k * 256, 256), 256)
        wt[s, :, at] = w[s, at, :].T
        return carry

    fwd = remote(c_out, c_in, hop_s.at[0], hop_r.at[0], ahead)
    bwd = remote(g_out, g_in, hop_s.at[1], hop_r.at[1], behind)

    def forward(s, carry, ready=True):
        block = c_out[...]
        cs[s] = block
        if ready:
            pre = jnp.dot(block, wt[s], preferred_element_type=F32)
        else:
            pre = lax.dot_general(block, w[s], (((1,), (1,)), ((), ())), preferred_element_type=F32)
        inv = lax.rsqrt(jnp.mean(pre * pre, axis=1, keepdims=True) + 1e-05)
        hat = pre * inv
        gain = gains[s]
        normed = hat * gain
        sig = 1.0 / (1.0 + jnp.exp(-normed))
        act = (normed * sig).astype(BF)
        c_out[...] = (block.astype(F32) + jnp.dot(act, w[s], preferred_element_type=F32)).astype(BF)
        xh[s] = hat
        dn[s] = sig * (1.0 + normed * (1.0 - sig)) * gain * inv
        acts[s, 0] = act[:, :HALF]
        acts[s, 1] = act[:, HALF:]
        return carry

    @pl.when(j == 0)
    def _():
        c_out[...] = b_ref[pl.ds(pl.multiple_of(x * T, T), T), :]
        lax.fori_loop(0, 4, lambda s, carry: forward(s, carry, ready=False), 0)
        fwd.start()
        lax.fori_loop(0, 40, transpose, 0)

    @pl.when(j > 0)
    def _():
        lax.fori_loop(0, 40, transpose, 0)
        fwd.wait_recv()
        c_out[...] = c_in[...]
        lax.fori_loop(0, 4, forward, 0)

    @pl.when((j > 0) & (j < 3))
    def _():
        fwd.start()

    ex = [
        remote(acts.at[:, 1 - c], acts_o, ex_s.at[0], ex_r.at[0], core_partner),
        remote(cs, cs_o, ex_s.at[1], ex_r.at[1], core_partner),
    ]

    @pl.when(j < 3)
    def _():
        ex[0].start()
        ex[1].start()

    for h, p in every:
        for step in range(6):
            gather(p, step, h).wait_send()
        across(p, 0, h).wait_send()
        across(p, 1, h).wait_send()

    @pl.when(j == 3)
    def _():
        g_out[...] = cot_ref[pl.ds(pl.multiple_of(x * T, T), T), :]

    @pl.when(j < 3)
    def _():
        bwd.wait_recv()
        g_out[...] = g_in[...]

    def ex_dpre(s):
        return remote(dpre.at[s, 1 - c], dpre_o.at[s], ex_s.at[2 + s], ex_r.at[2 + s], core_partner)

    def ex_grad(s):
        return remote(gs.at[s], gs_o.at[s], ex_s.at[6 + s], ex_r.at[6 + s], core_partner)

    def backward(i, carry):
        s = 3 - i
        grad = g_out[...]
        gs[s] = grad
        ex_grad(s).start()
        e = jnp.dot(grad, wt[s], preferred_element_type=F32) * dn[s]
        hat = xh[s]
        dp = (e - hat * jnp.mean(e * hat, axis=1, keepdims=True)).astype(BF)
        dpre[s, 0] = dp[:, :HALF]
        dpre[s, 1] = dp[:, HALF:]
        ex_dpre(s).start()
        grad_in = (grad.astype(F32) + jnp.dot(dp, w[s], preferred_element_type=F32)).astype(BF)
        g_out[...] = grad_in
        x_send[s] = grad_in
        return carry

    lax.fori_loop(0, 4, backward, 0)

    @pl.when(j > 0)
    def _():
        bwd.start()

    @pl.when(j == 3)
    def _():
        ex[0].start()
        ex[1].start()

    rows = pl.ds(pl.multiple_of(x * T, T), T)
    sg_ref[0, rows, :] = x_send[x]
    sg_copies = [
        remote(x_send.at[lax.rem(x + i, 4)], sg_ref.at[0, rows], sg_s.at[i - 1], sg_r.at[i - 1], beside[i - 1])
        for i in (1, 2, 3)
    ]
    for copy in sg_copies:
        copy.start()

    ex[0].wait_recv()
    ex[1].wait_recv()

    def outer(i, carry):
        s = 3 - i
        ex_grad(s).wait_recv()
        ex_dpre(s).wait_recv()
        right = jnp.concatenate([cs[s], cs_o[s], gs[s], gs_o[s]], axis=0)
        for zh in range(2):
            at = slice(zh * 640, zh * 640 + 640)
            left = jnp.concatenate(
                [dpre[s, c, :, at], dpre_o[s, :, at], acts[s, c, :, at], acts_o[s, :, at]], axis=0
            )
            grad = lax.dot_general(left, right, (((0,), (0,)), ((), ())), preferred_element_type=F32).astype(BF)
            for t in range(8):
                for p in range(PLANS):
                    g[p, place(p, s, 2 * zh + t // 4, t % 4, 0)] = grad[t * ROWS:(t + 1) * ROWS, p * LANES:(p + 1) * LANES]
        return carry

    lax.fori_loop(0, 4, outer, 0)

    own = [m - 64 * c for m in mine]

    def first(p, step):
        n = 1 << step
        return lax.div(own[p], n) * n

    def second(p, step):
        n = 1 << step
        return first(p, step) + n - 2 * n * lax.rem(lax.div(own[p], n), 2)

    def reduce(p, step, h):
        n = 1 << step
        return remote(
            g.at[p, pl.ds(second(p, step), n), STREAMS[h]],
            r.at[p, pl.ds(n - 1, n), STREAMS[h]],
            rs_s.at[step, p, h], rs_r.at[step, p, h], target(p, step),
        )

    for h, p in every:
        reduce(p, 5, h).start()
    for step in range(5, -1, -1):
        for h, p in every:
            n = 1 << step
            base = first(p, step)
            reduce(p, step, h).wait_recv()

            def add(start, count, p=p, h=h, n=n, base=base):
                def one(i, carry):
                    at = start + i
                    g[p, at, STREAMS[h]] = g[p, at, STREAMS[h]] + r[p, n - 1 + at - base, STREAMS[h]]
                    return carry

                lax.fori_loop(0, count, one, 0, unroll=min(count, 8))

            if step:
                add(second(p, step - 1), n // 2)
                reduce(p, step - 1, h).start()
                add(first(p, step - 1), n // 2)
            else:
                add(base, 1)

    for p in range(PLANS):
        wg_ref[0, :, p * LANES:(p + 1) * LANES] = g[p, own[p]].astype(F32) * (1.0 / math.sqrt(8192))

    for h, p in every:
        for step in range(6):
            reduce(p, step, h).wait_send()
    for copy in sg_copies:
        copy.wait()
    ex[0].wait_send()
    ex[1].wait_send()

    def sent(s, carry):
        ex_grad(s).wait_send()
        ex_dpre(s).wait_send()
        return carry

    lax.fori_loop(0, 4, sent, 0)

    @pl.when(j < 3)
    def _():
        fwd.wait_send()

    @pl.when(j > 0)
    def _():
        bwd.wait_send()


def shards(boundary_in, weights, gains, cotangent):
    vmem = pl.BlockSpec(memory_space=pltpu.VMEM)
    dma = pltpu.SemaphoreType.DMA
    return pl.pallas_call(
        kernel,
        out_shape=(
            jax.ShapeDtypeStruct((1, ROWS, C), F32),
            jax.ShapeDtypeStruct((1, 4 * T, C), BF),
        ),
        in_specs=[vmem] * 4,
        out_specs=(vmem, vmem),
        scratch_shapes=[
            pltpu.VMEM((PLANS, BLOCKS, ROWS, LANES), BF),
            pltpu.VMEM((PLANS, BLOCKS // 2 - 1, ROWS, LANES), BF),
            pltpu.VMEM((4, H, C), BF),
            pltpu.VMEM((4, C, H), BF),
            pltpu.VMEM((4, 1, H), F32),
            pltpu.VMEM((4, T, H), F32),
            pltpu.VMEM((4, T, H), F32),
            pltpu.VMEM((4, 2, T, HALF), BF),
            pltpu.VMEM((4, T, HALF), BF),
            pltpu.VMEM((4, 2, T, HALF), BF),
            pltpu.VMEM((4, T, HALF), BF),
            pltpu.VMEM((4, T, C), BF),
            pltpu.VMEM((4, T, C), BF),
            pltpu.VMEM((4, T, C), BF),
            pltpu.VMEM((4, T, C), BF),
            pltpu.VMEM((T, C), BF),
            pltpu.VMEM((T, C), BF),
            pltpu.VMEM((T, C), BF),
            pltpu.VMEM((T, C), BF),
            pltpu.VMEM((4, T, C), BF),
            dma((6, PLANS, 2)),
            dma((6, PLANS, 2)),
            dma((2, PLANS, 2)),
            dma((2, PLANS, 2)),
            dma((6, PLANS, 2)),
            dma((6, PLANS, 2)),
            dma((3,)),
            dma((3,)),
            dma((2,)),
            dma((2,)),
            dma((3,)),
            dma((3,)),
            dma((10,)),
            dma((10,)),
        ],
        compiler_params=pltpu.CompilerParams(
            collective_id=0, has_side_effects=True, vmem_limit_bytes=60 << 20
        ),
    )(boundary_in, weights, gains, cotangent)


def solution(mesh):
    return jax.shard_map(
        shards,
        mesh=mesh,
        in_specs=(P("dp", None), P("section", "dp", None), P("section", None), P("dp", None)),
        out_specs=(P("section", "dp", None), P("section", "dp", None)),
        check_vma=False,
    )
```

```python
import math

import jax
import jax.numpy as jnp
from jax import lax
from jax.experimental import pallas as pl
from jax.experimental.pallas import tpu as pltpu
from jax.sharding import PartitionSpec as P

MESH = pl.DeviceIdType.MESH
BF, F32 = jnp.bfloat16, jnp.float32
C, H, T = 640, 2560, 64
ROWS, LANES = 80, 128
PLANS = 5
BLOCKS = 128
HALF = H // 2
STREAMS = (slice(0, 48), slice(48, 80))
UNITS = [(h, p) for h in range(2) for p in range(PLANS)]

_FOUR, _ONE = ["xu", "yu", "za", "xv", "yv"], ["yu", "za", "yv"]
_TURN = [[0, 0], [1, 1], [2, 2], [0, 2], [1, 2]]
FOUR = [[["zb"] + [_FOUR[(p + i) % 5] for i in range(5)] for h in range(2)] for p in range(PLANS)]
ONE = [[["zb"] + [_ONE[(_TURN[p][h] + i) % 3] for i in range(3)] for h in range(2)] for p in range(PLANS)]


def place(order, s, zl, y, c):
    xu, yu = lax.div(s, 2), lax.div(y, 2)
    bits = {
        "xu": xu, "xv": lax.rem(lax.rem(s, 2) + xu, 2),
        "yu": yu, "yv": lax.rem(lax.rem(y, 2) + yu, 2),
        "za": lax.rem(zl, 2), "zb": lax.div(zl, 2),
    }
    at = c * (1 << len(order))
    for i, name in enumerate(order):
        at = at + bits[name] * (1 << i)
    return at


def kernel(b_ref, w_ref, gain_ref, cot_ref, wg_ref, sg_ref,
           g, r, w, wt, gains, xh, dn, acts, acts_o, dpre, dpre_o, cs, cs_o, gs, gs_o,
           c_in, c_out, g_in, g_out, x_send, x_back,
           ag_s, ag_r, co_s, co_r, rs_s, rs_r, gn_s, gn_r, hop_s, hop_r, sg_s, sg_r, ex_s, ex_r,
           up_s, up_r, down_s, down_r, relay_s, relay_r):
    sec, dp = lax.axis_index("section"), lax.axis_index("dp")
    j, x = lax.div(sec, 4), lax.rem(sec, 4)
    zl, y, c = lax.div(dp, 8), lax.rem(lax.div(dp, 2), 4), lax.rem(dp, 2)

    def device(j, x, zl, y, c):
        return (j * 4 + x, zl * 8 + y * 2 + c)

    def flip(v):
        return v + 1 - 2 * lax.rem(v, 2)

    partner = {
        "xu": device(j, 3 - x, zl, y, c),
        "xv": device(j, flip(x), zl, y, c),
        "yu": device(j, x, zl, 3 - y, c),
        "yv": device(j, x, zl, flip(y), c),
        "za": device(j, x, flip(zl), y, c),
        "zb": device(j, x, lax.rem(zl + 2, 4), y, c),
    }
    core_partner = device(j, x, zl, y, 1 - c)
    ahead = device(lax.rem(j + 1, 4), x, zl, y, c)
    behind = device(lax.rem(j + 3, 4), x, zl, y, c)
    beside = [device(j, lax.rem(x + i, 4), zl, y, c) for i in (1, 2, 3)]

    barrier = pltpu.get_barrier_semaphore()
    peers = list(partner.values()) + [core_partner, beside[1]]

    def greet(peer):
        pl.semaphore_signal(barrier, inc=1, device_id=peer, device_id_type=MESH)

    for peer in peers:
        greet(peer)

    def own_shard(orders, s):
        for h, p in UNITS:
            g[p, place(orders[p][h], s, zl, y, c), STREAMS[h]] = w_ref[0, STREAMS[h], p * LANES:(p + 1) * LANES]
        gains[s] = jnp.concatenate(
            [gain_ref[:, (2 * i + h) * ROWS:(2 * i + h + 1) * ROWS] for h in (0, 1) for i in range(16)], axis=1
        )

    last = device(0, 3, zl, y, c)

    @pl.when(j == 0)
    def _():
        own_shard(ONE, 0)
        pl.semaphore_wait(barrier, len(peers))

        @pl.when(x == 3)
        def _():
            for m in range(3):
                greet(device(1, m, zl, y, c))

    @pl.when(j > 0)
    def _():
        own_shard(FOUR, x)

        @pl.when((j == 1) & (x < 3))
        def _():
            pl.semaphore_wait(barrier, len(peers) + 2)

        @pl.when((j > 1) | (x == 3))
        def _():
            pl.semaphore_wait(barrier, len(peers) + 1)

        greet(behind)

    @pl.when(j < 3)
    def _():
        greet(ahead)

    def remote(src, dst, send, recv, to):
        return pltpu.make_async_remote_copy(
            src_ref=src, dst_ref=dst, send_sem=send, recv_sem=recv, device_id=to, device_id_type=MESH
        )

    def held(at, step):
        n = 1 << step
        return lax.div(at, n) * n

    def other(at, step):
        n = 1 << step
        return held(at, step) + n - 2 * n * lax.rem(lax.div(at, n), 2)

    def gathering(orders, s):
        steps = len(orders[0][0])

        def own(h, p):
            return place(orders[p][h], s, zl, y, c)

        def gather(h, p, step):
            part = g.at[p, pl.ds(held(own(h, p), step), 1 << step), STREAMS[h]]
            return remote(part, part, ag_s.at[step, p, h], ag_r.at[step, p, h], partner[orders[p][h][step]])

        def across(h, p, late):
            first = (other if late else held)(own(h, p), steps - 1)
            part = g.at[p, pl.ds(first, 1 << (steps - 1)), STREAMS[h]]
            return remote(part, part, co_s.at[late, p, h], co_r.at[late, p, h], core_partner)

        for unit in UNITS:
            gather(*unit, 0).start()
        for step in range(1, steps):
            for unit in UNITS:
                gather(*unit, step - 1).wait_recv()
                gather(*unit, step).start()
        for unit in UNITS:
            across(*unit, 0).start()
        for unit in UNITS:
            gather(*unit, steps - 1).wait_recv()
            across(*unit, 1).start()
        for unit in UNITS:
            across(*unit, 0).wait_recv()
            across(*unit, 1).wait_recv()

        def sends_done():
            for unit in UNITS:
                for step in range(steps):
                    gather(*unit, step).wait_send()
                across(*unit, 0).wait_send()
                across(*unit, 1).wait_send()

        return sends_done

    gain_copies = [
        remote(gains.at[x], gains.at[x], gn_s.at[i], gn_r.at[i], beside[i]) for i in range(3)
    ]

    def repack_four(i, carry):
        s, k = lax.div(i, 32), lax.rem(i, 32)
        c_, z_, y_ = lax.div(k, 16), lax.rem(lax.div(k, 4), 4), lax.rem(k, 4)
        for p in range(PLANS):
            at = place(FOUR[p][0], s, z_, y_, c_)
            w[s, pl.ds(pl.multiple_of(k * ROWS, 16), ROWS), p * LANES:(p + 1) * LANES] = g[p, at]
        return carry

    def repack_one(k, carry):
        c_, z_, y_ = lax.div(k, 16), lax.rem(lax.div(k, 4), 4), lax.rem(k, 4)
        for h, p in UNITS:
            rows = STREAMS[h]
            at = place(ONE[p][h], x, z_, y_, c_)
            to = pl.ds(pl.multiple_of(k * ROWS + rows.start, 16), rows.stop - rows.start)
            w[0, to, p * LANES:(p + 1) * LANES] = g[p, at, rows]
        return carry

    def transpose(i, carry):
        s, k = lax.div(i, 10), lax.rem(i, 10)
        at = pl.ds(pl.multiple_of(k * 256, 256), 256)
        wt[s, :, at] = w[s, at, :].T
        return carry

    fwd = remote(c_out, c_in, hop_s.at[0], hop_r.at[0], ahead)
    bwd = remote(g_out, g_in, hop_s.at[1], hop_r.at[1], behind)
    bwd_last = remote(g_out, gs.at[x], hop_s.at[1], down_r.at[x], last)

    def up(m):
        return remote(x_send.at[m], cs.at[m], up_s.at[m], up_r.at[m], device(j, lax.rem(x + 1, 4), zl, y, c))

    def down(m):
        return remote(x_back.at[m], gs.at[m], down_s.at[m], down_r.at[m], device(j, lax.rem(x + 3, 4), zl, y, c))

    def relay(m):
        return remote(x_send.at[m], c_in, relay_s.at[m], relay_r.at[0], device(j, m, zl, y, c))

    def forward(i, s, ready=True):
        block = cs[i]
        if ready:
            pre = jnp.dot(block, wt[s], preferred_element_type=F32)
        else:
            pre = lax.dot_general(block, w[s], (((1,), (1,)), ((), ())), preferred_element_type=F32)
        inv = lax.rsqrt(jnp.mean(pre * pre, axis=1, keepdims=True) + 1e-05)
        hat = pre * inv
        gain = gains[s]
        normed = hat * gain
        sig = 1.0 / (1.0 + jnp.exp(-normed))
        act = (normed * sig).astype(BF)
        xh[i] = hat
        dn[i] = sig * (1.0 + normed * (1.0 - sig)) * gain * inv
        acts[i, 0] = act[:, :HALF]
        acts[i, 1] = act[:, HALF:]
        return (block.astype(F32) + jnp.dot(act, w[s], preferred_element_type=F32)).astype(BF)

    @pl.when(j == 0)
    def _():
        sends_done = gathering(ONE, x)
        lax.fori_loop(0, 32, repack_one, 0)
        lax.fori_loop(0, 10, transpose, 0)

        @pl.when(x == 0)
        def _():
            for m in range(4):
                cs[m] = b_ref[m * T:(m + 1) * T, :]

        def step(m, carry):
            @pl.when(x > 0)
            def _():
                up(m).wait_recv()

            x_send[m] = forward(m, 0)

            @pl.when(x < 3)
            def _():
                up(m).start()

            @pl.when((x == 3) & (m < 3))
            def _():
                relay(m).start()

            return carry

        lax.fori_loop(0, 4, step, 0)

        @pl.when(x == 3)
        def _():
            c_out[...] = x_send[3]

        @pl.when(x < 3)
        def _():
            relay(0).wait_recv()
            c_out[...] = c_in[...]

        pl.semaphore_wait(barrier, 1)
        fwd.start()
        sends_done()

    @pl.when(j > 0)
    def _():
        for copy in gain_copies:
            copy.start()
        sends_done = gathering(FOUR, x)
        for copy in gain_copies:
            copy.wait()
        lax.fori_loop(0, 4 * 32, repack_four, 0)

        def step(s, carry, ready=True):
            cs[s] = c_out[...]
            c_out[...] = forward(s, s, ready)
            return carry

        @pl.when(j == 1)
        def _():
            fwd.wait_recv()
            c_out[...] = c_in[...]
            lax.fori_loop(0, 4, lambda s, carry: step(s, carry, False), 0)
            pl.semaphore_wait(barrier, 1)
            fwd.start()
            lax.fori_loop(0, 40, transpose, 0)

        @pl.when(j > 1)
        def _():
            lax.fori_loop(0, 40, transpose, 0)
            fwd.wait_recv()
            c_out[...] = c_in[...]
            lax.fori_loop(0, 4, step, 0)

            @pl.when(j < 3)
            def _():
                pl.semaphore_wait(barrier, 1)
                fwd.start()

        sends_done()

    ex = [
        remote(acts.at[:, 1 - c], acts_o, ex_s.at[0], ex_r.at[0], core_partner),
        remote(cs, cs_o, ex_s.at[1], ex_r.at[1], core_partner),
    ]

    @pl.when(j < 3)
    def _():
        ex[0].start()
        ex[1].start()

    def ex_dpre(s):
        return remote(dpre.at[s, 1 - c], dpre_o.at[s], ex_s.at[2 + s], ex_r.at[2 + s], core_partner)

    def ex_grad(s):
        return remote(gs.at[s], gs_o.at[s], ex_s.at[6 + s], ex_r.at[6 + s], core_partner)

    def backward(i, s):
        grad = gs[i]
        e = jnp.dot(grad, wt[s], preferred_element_type=F32) * dn[i]
        hat = xh[i]
        dp = (e - hat * jnp.mean(e * hat, axis=1, keepdims=True)).astype(BF)
        dpre[i, 0] = dp[:, :HALF]
        dpre[i, 1] = dp[:, HALF:]
        return (grad.astype(F32) + jnp.dot(dp, w[s], preferred_element_type=F32)).astype(BF)

    rows = pl.ds(pl.multiple_of(x * T, T), T)
    sg_copies = [
        remote(x_back.at[lax.rem(x + i, 4)], sg_ref.at[0, rows], sg_s.at[i - 1], sg_r.at[i - 1], beside[i - 1])
        for i in (1, 2, 3)
    ]

    @pl.when(j == 0)
    def _():
        def step(m, carry):
            down(m).wait_recv()
            grad = backward(m, 0)
            x_back[m] = grad

            @pl.when(x > 0)
            def _():
                down(m).start()

            ex_grad(m).start()
            ex_dpre(m).start()
            sg_ref[0, pl.ds(pl.multiple_of(m * T, T), T), :] = grad
            return carry

        lax.fori_loop(0, 4, step, 0)

    @pl.when(j > 0)
    def _():
        @pl.when(j == 3)
        def _():
            g_out[...] = cot_ref[rows, :]

        @pl.when(j < 3)
        def _():
            bwd.wait_recv()
            g_out[...] = g_in[...]

        def step(i, carry):
            s = 3 - i
            gs[s] = g_out[...]
            grad = backward(s, s)
            g_out[...] = grad

            @pl.when((i == 3) & (j == 1))
            def _():
                bwd_last.start()

            @pl.when((i == 3) & (j > 1))
            def _():
                bwd.start()

            x_back[s] = grad
            ex_grad(s).start()
            ex_dpre(s).start()
            return carry

        lax.fori_loop(0, 4, step, 0)

        sg_ref[0, rows, :] = x_back[x]
        for copy in sg_copies:
            copy.start()

    @pl.when(j == 3)
    def _():
        ex[0].start()
        ex[1].start()

    ex[0].wait_recv()
    ex[1].wait_recv()

    def left_of(i, at):
        return [dpre[i, c, :, at], dpre_o[i, :, at], acts[i, c, :, at], acts_o[i, :, at]]

    def right_of(i):
        return [cs[i], cs_o[i], gs[i], gs_o[i]]

    def outer(left, right):
        left, right = jnp.concatenate(left, axis=0), jnp.concatenate(right, axis=0)
        return lax.dot_general(left, right, (((0,), (0,)), ((), ())), preferred_element_type=F32).astype(BF)

    def summing(orders, s):
        steps = len(orders[0][0])

        def own(h, p):
            return place(orders[p][h], s, zl, y, 0)

        def reduce(h, p, step):
            n = 1 << step
            return remote(
                g.at[p, pl.ds(other(own(h, p), step), n), STREAMS[h]],
                r.at[p, pl.ds(n - 1, n), STREAMS[h]],
                rs_s.at[step, p, h], rs_r.at[step, p, h], partner[orders[p][h][step]],
            )

        for unit in UNITS:
            reduce(*unit, steps - 1).start()
        for step in range(steps - 1, -1, -1):
            for h, p in UNITS:
                n = 1 << step
                base = held(own(h, p), step)
                reduce(h, p, step).wait_recv()

                def add(start, count, p=p, h=h, n=n, base=base):
                    def one(i, carry):
                        at = start + i
                        g[p, at, STREAMS[h]] = g[p, at, STREAMS[h]] + r[p, n - 1 + at - base, STREAMS[h]]
                        return carry

                    lax.fori_loop(0, count, one, 0, unroll=min(count, 8))

                if step:
                    add(other(own(h, p), step - 1), n // 2)
                    reduce(h, p, step - 1).start()
                    add(held(own(h, p), step - 1), n // 2)
                else:
                    add(base, 1)

        for h, p in UNITS:
            total = g[p, own(h, p), STREAMS[h]].astype(F32)
            wg_ref[0, STREAMS[h], p * LANES:(p + 1) * LANES] = total * (1.0 / math.sqrt(8192))
        for unit in UNITS:
            for step in range(steps):
                reduce(*unit, step).wait_send()

    @pl.when(j == 0)
    def _():
        right = []
        for m in range(4):
            ex_grad(m).wait_recv()
            ex_dpre(m).wait_recv()
            right += right_of(m)
        for zh in range(2):
            at = slice(zh * 640, zh * 640 + 640)
            grad = outer([v for m in range(4) for v in left_of(m, at)], right)
            for t in range(8):
                for h, p in UNITS:
                    rows = STREAMS[h]
                    to = place(ONE[p][h], x, 2 * zh + t // 4, t % 4, 0)
                    g[p, to, rows] = grad[t * ROWS + rows.start:t * ROWS + rows.stop, p * LANES:(p + 1) * LANES]
        summing(ONE, x)

    @pl.when(j > 0)
    def _():
        def section(i, carry):
            s = 3 - i
            ex_grad(s).wait_recv()
            ex_dpre(s).wait_recv()
            for zh in range(2):
                grad = outer(left_of(s, slice(zh * 640, zh * 640 + 640)), right_of(s))
                for t in range(8):
                    for p in range(PLANS):
                        to = place(FOUR[p][0], s, 2 * zh + t // 4, t % 4, 0)
                        g[p, to] = grad[t * ROWS:(t + 1) * ROWS, p * LANES:(p + 1) * LANES]
            return carry

        lax.fori_loop(0, 4, section, 0)
        summing(FOUR, x)
        for copy in sg_copies:
            copy.wait()

    ex[0].wait_send()
    ex[1].wait_send()

    def sent(s, carry):
        ex_grad(s).wait_send()
        ex_dpre(s).wait_send()
        return carry

    lax.fori_loop(0, 4, sent, 0)

    @pl.when(j < 3)
    def _():
        fwd.wait_send()

    @pl.when(j > 0)
    def _():
        bwd.wait_send()

    @pl.when(j == 0)
    def _():
        def sent(m, carry):
            @pl.when(x < 3)
            def _():
                up(m).wait_send()

            @pl.when((x == 3) & (m < 3))
            def _():
                relay(m).wait_send()

            @pl.when(x > 0)
            def _():
                down(m).wait_send()

            return carry

        lax.fori_loop(0, 4, sent, 0)


def shards(boundary_in, weights, gains, cotangent):
    vmem = pl.BlockSpec(memory_space=pltpu.VMEM)
    dma = pltpu.SemaphoreType.DMA
    return pl.pallas_call(
        kernel,
        out_shape=(
            jax.ShapeDtypeStruct((1, ROWS, C), F32),
            jax.ShapeDtypeStruct((1, 4 * T, C), BF),
        ),
        in_specs=[vmem] * 4,
        out_specs=(vmem, vmem),
        scratch_shapes=[
            pltpu.VMEM((PLANS, BLOCKS, ROWS, LANES), BF),
            pltpu.VMEM((PLANS, BLOCKS // 2 - 1, ROWS, LANES), BF),
            pltpu.VMEM((4, H, C), BF),
            pltpu.VMEM((4, C, H), BF),
            pltpu.VMEM((4, 1, H), F32),
            pltpu.VMEM((4, T, H), F32),
            pltpu.VMEM((4, T, H), F32),
            pltpu.VMEM((4, 2, T, HALF), BF),
            pltpu.VMEM((4, T, HALF), BF),
            pltpu.VMEM((4, 2, T, HALF), BF),
            pltpu.VMEM((4, T, HALF), BF),
            pltpu.VMEM((4, T, C), BF),
            pltpu.VMEM((4, T, C), BF),
            pltpu.VMEM((4, T, C), BF),
            pltpu.VMEM((4, T, C), BF),
            pltpu.VMEM((T, C), BF),
            pltpu.VMEM((T, C), BF),
            pltpu.VMEM((T, C), BF),
            pltpu.VMEM((T, C), BF),
            pltpu.VMEM((4, T, C), BF),
            pltpu.VMEM((4, T, C), BF),
            dma((6, PLANS, 2)),
            dma((6, PLANS, 2)),
            dma((2, PLANS, 2)),
            dma((2, PLANS, 2)),
            dma((6, PLANS, 2)),
            dma((6, PLANS, 2)),
            dma((3,)),
            dma((3,)),
            dma((2,)),
            dma((2,)),
            dma((3,)),
            dma((3,)),
            dma((10,)),
            dma((10,)),
            dma((4,)),
            dma((4,)),
            dma((4,)),
            dma((4,)),
            dma((3,)),
            dma((1,)),
        ],
        compiler_params=pltpu.CompilerParams(
            collective_id=0, has_side_effects=True, vmem_limit_bytes=60 << 20
        ),
    )(boundary_in, weights, gains, cotangent)


def solution(mesh):
    return jax.shard_map(
        shards,
        mesh=mesh,
        in_specs=(P("dp", None), P("section", "dp", None), P("section", None), P("dp", None)),
        out_specs=(P("section", "dp", None), P("section", "dp", None)),
        check_vma=False,
    )
```

```python
import math

import jax
import jax.numpy as jnp
from jax import lax
from jax.experimental import pallas as pl
from jax.experimental.pallas import tpu as pltpu
from jax.sharding import PartitionSpec as P

MESH = pl.DeviceIdType.MESH
BF, F32 = jnp.bfloat16, jnp.float32
C, H, T = 640, 2560, 64
ROWS, LANES = 80, 128
PLANS = 5
BLOCKS = 128
HALF = H // 2
STREAMS = (slice(0, 48), slice(48, 80))
COLS = (slice(0, 256), slice(256, C))
UNITS = [(h, p) for h in range(2) for p in range(PLANS)]

_FOUR, _ONE = ["xu", "yu", "za", "xv", "yv"], ["yu", "za", "yv"]
_TURN = [[0, 0], [1, 1], [2, 2], [0, 2], [1, 2]]
FOUR = [[["zb"] + [_FOUR[(p + i) % 5] for i in range(5)] for h in range(2)] for p in range(PLANS)]
ONE = [[["zb"] + [_ONE[(_TURN[p][h] + i) % 3] for i in range(3)] for h in range(2)] for p in range(PLANS)]


def place(order, s, zl, y, c):
    xu, yu = lax.div(s, 2), lax.div(y, 2)
    bits = {
        "xu": xu, "xv": lax.rem(lax.rem(s, 2) + xu, 2),
        "yu": yu, "yv": lax.rem(lax.rem(y, 2) + yu, 2),
        "za": lax.rem(zl, 2), "zb": lax.div(zl, 2),
    }
    at = c * (1 << len(order))
    for i, name in enumerate(order):
        at = at + bits[name] * (1 << i)
    return at


def kernel(b_ref, w_ref, gain_ref, cot_ref, wg_ref, sg_ref,
           g, r, w, wt, gains, xh, dn, acts, acts_o, dpre, dpre_o, cs, cs_o, gs, gs_o,
           c_in, c_out, g_out, x_send, x_back,
           ag_s, ag_r, co_s, co_r, rs_s, rs_r, gn_s, gn_r, hop_s, sg_s, sg_r, ex_s, ex_r,
           up_s, up_r, down_s, down_r, relay_s, relay_r):
    sec, dp = lax.axis_index("section"), lax.axis_index("dp")
    j, x = lax.div(sec, 4), lax.rem(sec, 4)
    zl, y, c = lax.div(dp, 8), lax.rem(lax.div(dp, 2), 4), lax.rem(dp, 2)

    def device(j, x, zl, y, c):
        return (j * 4 + x, zl * 8 + y * 2 + c)

    def flip(v):
        return v + 1 - 2 * lax.rem(v, 2)

    partner = {
        "xu": device(j, 3 - x, zl, y, c),
        "xv": device(j, flip(x), zl, y, c),
        "yu": device(j, x, zl, 3 - y, c),
        "yv": device(j, x, zl, flip(y), c),
        "za": device(j, x, flip(zl), y, c),
        "zb": device(j, x, lax.rem(zl + 2, 4), y, c),
    }
    core_partner = device(j, x, zl, y, 1 - c)
    ahead = device(lax.rem(j + 1, 4), x, zl, y, c)
    behind = device(lax.rem(j + 3, 4), x, zl, y, c)
    beside = [device(j, lax.rem(x + i, 4), zl, y, c) for i in (1, 2, 3)]

    barrier = pltpu.get_barrier_semaphore()
    peers = list(partner.values()) + [core_partner, beside[1]]

    def greet(peer):
        pl.semaphore_signal(barrier, inc=1, device_id=peer, device_id_type=MESH)

    for peer in peers:
        greet(peer)

    def own_shard(orders, s):
        for h, p in UNITS:
            g[p, place(orders[p][h], s, zl, y, c), STREAMS[h]] = w_ref[0, STREAMS[h], p * LANES:(p + 1) * LANES]
        gains[s] = jnp.concatenate(
            [gain_ref[:, (2 * i + h) * ROWS:(2 * i + h + 1) * ROWS] for h in (0, 1) for i in range(16)], axis=1
        )

    last = device(0, 3, zl, y, c)

    @pl.when(j == 0)
    def _():
        own_shard(ONE, 0)
        pl.semaphore_wait(barrier, len(peers))

        @pl.when(x == 3)
        def _():
            for m in range(3):
                greet(device(1, m, zl, y, c))

    @pl.when(j > 0)
    def _():
        own_shard(FOUR, x)

        @pl.when((j == 1) & (x < 3))
        def _():
            pl.semaphore_wait(barrier, len(peers) + 2)

        @pl.when((j > 1) | (x == 3))
        def _():
            pl.semaphore_wait(barrier, len(peers) + 1)

        greet(behind)

    @pl.when(j < 3)
    def _():
        greet(ahead)

    def remote(src, dst, send, recv, to):
        return pltpu.make_async_remote_copy(
            src_ref=src, dst_ref=dst, send_sem=send, recv_sem=recv, device_id=to, device_id_type=MESH
        )

    def held(at, step):
        n = 1 << step
        return lax.div(at, n) * n

    def other(at, step):
        n = 1 << step
        return held(at, step) + n - 2 * n * lax.rem(lax.div(at, n), 2)

    def gathering(orders, s):
        steps = len(orders[0][0])

        def own(h, p):
            return place(orders[p][h], s, zl, y, c)

        def gather(h, p, step, late):
            if step:
                first, n = (other if late else held)(own(h, p), step - 1), 1 << (step - 1)
            else:
                first, n = own(h, p), 1
            part = g.at[p, pl.ds(first, n), STREAMS[h]]
            return remote(part, part, ag_s.at[step, late, p, h], ag_r.at[step, late, p, h], partner[orders[p][h][step]])

        def arrive(h, p, step):
            if step:
                gather(h, p, step, 0).wait_recv()
            gather(h, p, step, 1).wait_recv()

        def across(h, p, late):
            first = (other if late else held)(own(h, p), steps - 1)
            part = g.at[p, pl.ds(first, 1 << (steps - 1)), STREAMS[h]]
            return remote(part, part, co_s.at[late, p, h], co_r.at[late, p, h], core_partner)

        for unit in UNITS:
            gather(*unit, 0, 1).start()
        for unit in UNITS:
            gather(*unit, 1, 0).start()
        for step in range(1, steps):
            for unit in UNITS:
                arrive(*unit, step - 1)
                gather(*unit, step, 1).start()
                if step + 1 < steps:
                    gather(*unit, step + 1, 0).start()
        for unit in UNITS:
            across(*unit, 0).start()
        for unit in UNITS:
            arrive(*unit, steps - 1)
            across(*unit, 1).start()
        for unit in UNITS:
            across(*unit, 0).wait_recv()
            across(*unit, 1).wait_recv()

        def sends_done():
            for unit in UNITS:
                for step in range(steps):
                    if step:
                        gather(*unit, step, 0).wait_send()
                    gather(*unit, step, 1).wait_send()
                across(*unit, 0).wait_send()
                across(*unit, 1).wait_send()

        return sends_done

    gain_copies = [
        remote(gains.at[x], gains.at[x], gn_s.at[i], gn_r.at[i], beside[i]) for i in range(3)
    ]

    def repack_four(i, carry):
        s, k = lax.div(i, 32), lax.rem(i, 32)
        c_, z_, y_ = lax.div(k, 16), lax.rem(lax.div(k, 4), 4), lax.rem(k, 4)
        for p in range(PLANS):
            at = place(FOUR[p][0], s, z_, y_, c_)
            w[s, pl.ds(pl.multiple_of(k * ROWS, 16), ROWS), p * LANES:(p + 1) * LANES] = g[p, at]
        return carry

    def repack_one(k, carry):
        c_, z_, y_ = lax.div(k, 16), lax.rem(lax.div(k, 4), 4), lax.rem(k, 4)
        for h, p in UNITS:
            rows = STREAMS[h]
            at = place(ONE[p][h], x, z_, y_, c_)
            to = pl.ds(pl.multiple_of(k * ROWS + rows.start, 16), rows.stop - rows.start)
            w[0, to, p * LANES:(p + 1) * LANES] = g[p, at, rows]
        return carry

    def transpose(i, carry):
        s, k = lax.div(i, 10), lax.rem(i, 10)
        at = pl.ds(pl.multiple_of(k * 256, 256), 256)
        wt[s, :, at] = w[s, at, :].T
        return carry

    def hop(src, dst, sems, i, part, to):
        cols = COLS[part]
        return remote(src.at[:, cols], dst.at[:, cols], sems[0].at[i, part], sems[1].at[i, part], to)

    UP, DOWN = (up_s, up_r), (down_s, down_r)

    def fwd(part, src):
        return hop(src, cs.at[0], (hop_s, up_r), 0, part, ahead)

    def bwd(part):
        return hop(g_out, gs.at[3], (hop_s, down_r), 1, part, behind)

    def bwd_last(part):
        cols = COLS[part]
        return remote(g_out.at[:, cols], gs.at[x, :, cols], hop_s.at[1, part], down_r.at[x, part], last)

    def up(m, part):
        return hop(x_send.at[m], cs.at[m], UP, m, part, device(j, lax.rem(x + 1, 4), zl, y, c))

    def down(m, part):
        return hop(x_back.at[m], gs.at[m], DOWN, m, part, device(j, lax.rem(x + 3, 4), zl, y, c))

    def relay(m, part):
        cols = COLS[part]
        return remote(x_send.at[m, :, cols], c_in.at[:, cols], relay_s.at[m, part], relay_r.at[0, part], device(j, m, zl, y, c))

    def by_parts(value, weight, arrived):
        if arrived is None:
            return jnp.dot(value[...], weight[...], preferred_element_type=F32)
        arrived(0)
        total = jnp.dot(value[:, COLS[0]], weight[COLS[0], :], preferred_element_type=F32)
        arrived(1)
        return total + jnp.dot(value[:, COLS[1]], weight[COLS[1], :], preferred_element_type=F32)

    def leave(block, change, s, send):
        for part, cols in enumerate(COLS):
            out = block[:, cols].astype(F32) + jnp.dot(change, w[s, :, cols], preferred_element_type=F32)
            send(part, out.astype(BF))

    def forward(i, s, send, arrived=None, ready=True):
        if ready:
            pre = by_parts(cs.at[i], wt.at[s], arrived)
        else:
            if arrived is not None:
                arrived(0)
                arrived(1)
            pre = lax.dot_general(cs[i], w[s], (((1,), (1,)), ((), ())), preferred_element_type=F32)
        inv = lax.rsqrt(jnp.mean(pre * pre, axis=1, keepdims=True) + 1e-05)
        hat = pre * inv
        gain = gains[s]
        normed = hat * gain
        sig = 1.0 / (1.0 + jnp.exp(-normed))
        act = (normed * sig).astype(BF)
        leave(cs.at[i], act, s, send)
        xh[i] = hat
        dn[i] = sig * (1.0 + normed * (1.0 - sig)) * gain * inv
        acts[i, 0] = act[:, :HALF]
        acts[i, 1] = act[:, HALF:]

    @pl.when(j == 0)
    def _():
        sends_done = gathering(ONE, x)
        lax.fori_loop(0, 32, repack_one, 0)
        lax.fori_loop(0, 10, transpose, 0)

        @pl.when(x == 0)
        def _():
            for m in range(4):
                cs[m] = b_ref[m * T:(m + 1) * T, :]

        def step(m, carry):
            def arrived(part):
                @pl.when(x > 0)
                def _():
                    up(m, part).wait_recv()

            def send(part, value):
                x_send[m, :, COLS[part]] = value

                @pl.when(x < 3)
                def _():
                    up(m, part).start()

                @pl.when((x == 3) & (m < 3))
                def _():
                    relay(m, part).start()

            forward(m, 0, send, arrived)
            return carry

        lax.fori_loop(0, 4, step, 0)
        pl.semaphore_wait(barrier, 1)
        for part in range(2):
            @pl.when(x == 3)
            def _():
                fwd(part, x_send.at[3]).start()

            @pl.when(x < 3)
            def _():
                relay(0, part).wait_recv()
                fwd(part, c_in).start()

        sends_done()

    @pl.when(j > 0)
    def _():
        for copy in gain_copies:
            copy.start()
        sends_done = gathering(FOUR, x)
        for copy in gain_copies:
            copy.wait()
        lax.fori_loop(0, 4 * 32, repack_four, 0)

        def arrived(part):
            fwd(part, c_out).wait_recv()

        def stage(ready):
            def within(s, carry):
                def send(part, value):
                    cs[s + 1, :, COLS[part]] = value

                forward(s, s, send, ready=ready)
                return carry

            def send(part, value):
                c_out[:, COLS[part]] = value
                fwd(part, c_out).start()

            def end(part, value):
                pass

            def first(part, value):
                cs[1, :, COLS[part]] = value

            forward(0, 0, first, arrived, ready)
            lax.fori_loop(1, 3, within, 0)

            @pl.when(j < 3)
            def _():
                pl.semaphore_wait(barrier, 1)
                forward(3, 3, send, ready=ready)

            if ready:
                @pl.when(j == 3)
                def _():
                    forward(3, 3, end)

        @pl.when(j == 1)
        def _():
            stage(False)
            lax.fori_loop(0, 40, transpose, 0)

        @pl.when(j > 1)
        def _():
            lax.fori_loop(0, 40, transpose, 0)
            stage(True)

        sends_done()

    ex = [
        remote(acts.at[:, 1 - c], acts_o, ex_s.at[0], ex_r.at[0], core_partner),
        remote(cs, cs_o, ex_s.at[1], ex_r.at[1], core_partner),
    ]

    @pl.when(j < 3)
    def _():
        ex[0].start()
        ex[1].start()

    def ex_dpre(s):
        return remote(dpre.at[s, 1 - c], dpre_o.at[s], ex_s.at[2 + s], ex_r.at[2 + s], core_partner)

    def ex_grad(s):
        return remote(gs.at[s], gs_o.at[s], ex_s.at[6 + s], ex_r.at[6 + s], core_partner)

    def backward(i, s, send, arrived=None):
        e = by_parts(gs.at[i], wt.at[s], arrived) * dn[i]
        hat = xh[i]
        dp = (e - hat * jnp.mean(e * hat, axis=1, keepdims=True)).astype(BF)
        leave(gs.at[i], dp, s, send)
        dpre[i, 0] = dp[:, :HALF]
        dpre[i, 1] = dp[:, HALF:]
        ex_grad(i).start()
        ex_dpre(i).start()

    rows = pl.ds(pl.multiple_of(x * T, T), T)
    sg_copies = [
        remote(x_back.at[lax.rem(x + i, 4)], sg_ref.at[0, rows], sg_s.at[i - 1], sg_r.at[i - 1], beside[i - 1])
        for i in (1, 2, 3)
    ]

    @pl.when(j == 0)
    def _():
        def step(m, carry):
            def arrived(part):
                down(m, part).wait_recv()

            def send(part, value):
                x_back[m, :, COLS[part]] = value

                @pl.when(x > 0)
                def _():
                    down(m, part).start()

            backward(m, 0, send, arrived)
            sg_ref[0, pl.ds(pl.multiple_of(m * T, T), T), :] = x_back[m]
            return carry

        lax.fori_loop(0, 4, step, 0)

    @pl.when(j > 0)
    def _():
        @pl.when(j == 3)
        def _():
            gs[3] = cot_ref[rows, :]

        def arrived(part):
            @pl.when(j < 3)
            def _():
                bwd(part).wait_recv()

        def first(part, value):
            gs[2, :, COLS[part]] = value
            x_back[3, :, COLS[part]] = value

        def step(i, carry):
            s = 3 - i

            def send(part, value):
                gs[s - 1, :, COLS[part]] = value
                x_back[s, :, COLS[part]] = value

            backward(s, s, send)
            return carry

        def out(part, value):
            g_out[:, COLS[part]] = value

            @pl.when(j == 1)
            def _():
                bwd_last(part).start()

            @pl.when(j > 1)
            def _():
                bwd(part).start()

            x_back[0, :, COLS[part]] = value

        backward(3, 3, first, arrived)
        lax.fori_loop(1, 3, step, 0)
        backward(0, 0, out)
        sg_ref[0, rows, :] = x_back[x]
        for copy in sg_copies:
            copy.start()

    @pl.when(j == 3)
    def _():
        ex[0].start()
        ex[1].start()

    ex[0].wait_recv()
    ex[1].wait_recv()

    def left_of(i, at):
        return [dpre[i, c, :, at], dpre_o[i, :, at], acts[i, c, :, at], acts_o[i, :, at]]

    def right_of(i):
        return [cs[i], cs_o[i], gs[i], gs_o[i]]

    def outer(left, right):
        left, right = jnp.concatenate(left, axis=0), jnp.concatenate(right, axis=0)
        return lax.dot_general(left, right, (((0,), (0,)), ((), ())), preferred_element_type=F32).astype(BF)

    def summing(orders, s):
        steps = len(orders[0][0])

        def own(h, p):
            return place(orders[p][h], s, zl, y, 0)

        def reduce(h, p, step):
            n = 1 << step
            return remote(
                g.at[p, pl.ds(other(own(h, p), step), n), STREAMS[h]],
                r.at[p, pl.ds(n - 1, n), STREAMS[h]],
                rs_s.at[step, p, h], rs_r.at[step, p, h], partner[orders[p][h][step]],
            )

        for unit in UNITS:
            reduce(*unit, steps - 1).start()
        for step in range(steps - 1, -1, -1):
            for h, p in UNITS:
                n = 1 << step
                base = held(own(h, p), step)
                reduce(h, p, step).wait_recv()

                def add(start, count, p=p, h=h, n=n, base=base):
                    def one(i, carry):
                        at = start + i
                        g[p, at, STREAMS[h]] = g[p, at, STREAMS[h]] + r[p, n - 1 + at - base, STREAMS[h]]
                        return carry

                    lax.fori_loop(0, count, one, 0, unroll=min(count, 8))

                if step:
                    add(other(own(h, p), step - 1), n // 2)
                    reduce(h, p, step - 1).start()
                    add(held(own(h, p), step - 1), n // 2)
                else:
                    add(base, 1)

        for h, p in UNITS:
            total = g[p, own(h, p), STREAMS[h]].astype(F32)
            wg_ref[0, STREAMS[h], p * LANES:(p + 1) * LANES] = total * (1.0 / math.sqrt(8192))
        for unit in UNITS:
            for step in range(steps):
                reduce(*unit, step).wait_send()

    @pl.when(j == 0)
    def _():
        right = []
        for m in range(4):
            ex_grad(m).wait_recv()
            ex_dpre(m).wait_recv()
            right += right_of(m)
        for zh in range(2):
            at = slice(zh * 640, zh * 640 + 640)
            grad = outer([v for m in range(4) for v in left_of(m, at)], right)
            for t in range(8):
                for h, p in UNITS:
                    rows = STREAMS[h]
                    to = place(ONE[p][h], x, 2 * zh + t // 4, t % 4, 0)
                    g[p, to, rows] = grad[t * ROWS + rows.start:t * ROWS + rows.stop, p * LANES:(p + 1) * LANES]
        summing(ONE, x)

    @pl.when(j > 0)
    def _():
        def section(i, carry):
            s = 3 - i
            ex_grad(s).wait_recv()
            ex_dpre(s).wait_recv()
            for zh in range(2):
                grad = outer(left_of(s, slice(zh * 640, zh * 640 + 640)), right_of(s))
                for t in range(8):
                    for p in range(PLANS):
                        to = place(FOUR[p][0], s, 2 * zh + t // 4, t % 4, 0)
                        g[p, to] = grad[t * ROWS:(t + 1) * ROWS, p * LANES:(p + 1) * LANES]
            return carry

        lax.fori_loop(0, 4, section, 0)
        summing(FOUR, x)
        for copy in sg_copies:
            copy.wait()

    ex[0].wait_send()
    ex[1].wait_send()

    def sent(s, carry):
        ex_grad(s).wait_send()
        ex_dpre(s).wait_send()
        return carry

    lax.fori_loop(0, 4, sent, 0)

    for part in range(2):
        @pl.when(j < 3)
        def _():
            fwd(part, c_out).wait_send()

        @pl.when(j > 0)
        def _():
            bwd(part).wait_send()

    @pl.when(j == 0)
    def _():
        def sent(m, carry):
            for part in range(2):
                @pl.when(x < 3)
                def _():
                    up(m, part).wait_send()

                @pl.when((x == 3) & (m < 3))
                def _():
                    relay(m, part).wait_send()

                @pl.when(x > 0)
                def _():
                    down(m, part).wait_send()

            return carry

        lax.fori_loop(0, 4, sent, 0)


def shards(boundary_in, weights, gains, cotangent):
    vmem = pl.BlockSpec(memory_space=pltpu.VMEM)
    dma = pltpu.SemaphoreType.DMA
    return pl.pallas_call(
        kernel,
        out_shape=(
            jax.ShapeDtypeStruct((1, ROWS, C), F32),
            jax.ShapeDtypeStruct((1, 4 * T, C), BF),
        ),
        in_specs=[vmem] * 4,
        out_specs=(vmem, vmem),
        scratch_shapes=[
            pltpu.VMEM((PLANS, BLOCKS, ROWS, LANES), BF),
            pltpu.VMEM((PLANS, BLOCKS // 2 - 1, ROWS, LANES), BF),
            pltpu.VMEM((4, H, C), BF),
            pltpu.VMEM((4, C, H), BF),
            pltpu.VMEM((4, 1, H), F32),
            pltpu.VMEM((4, T, H), F32),
            pltpu.VMEM((4, T, H), F32),
            pltpu.VMEM((4, 2, T, HALF), BF),
            pltpu.VMEM((4, T, HALF), BF),
            pltpu.VMEM((4, 2, T, HALF), BF),
            pltpu.VMEM((4, T, HALF), BF),
            pltpu.VMEM((4, T, C), BF),
            pltpu.VMEM((4, T, C), BF),
            pltpu.VMEM((4, T, C), BF),
            pltpu.VMEM((4, T, C), BF),
            pltpu.VMEM((T, C), BF),
            pltpu.VMEM((T, C), BF),
            pltpu.VMEM((T, C), BF),
            pltpu.VMEM((4, T, C), BF),
            pltpu.VMEM((4, T, C), BF),
            dma((6, 2, PLANS, 2)),
            dma((6, 2, PLANS, 2)),
            dma((2, PLANS, 2)),
            dma((2, PLANS, 2)),
            dma((6, PLANS, 2)),
            dma((6, PLANS, 2)),
            dma((3,)),
            dma((3,)),
            dma((2, 2)),
            dma((3,)),
            dma((3,)),
            dma((10,)),
            dma((10,)),
            dma((4, 2)),
            dma((4, 2)),
            dma((4, 2)),
            dma((4, 2)),
            dma((3, 2)),
            dma((1, 2)),
        ],
        compiler_params=pltpu.CompilerParams(
            collective_id=0, has_side_effects=True, vmem_limit_bytes=60 << 20
        ),
    )(boundary_in, weights, gains, cotangent)


def solution(mesh):
    return jax.shard_map(
        shards,
        mesh=mesh,
        in_specs=(P("dp", None), P("section", "dp", None), P("section", None), P("dp", None)),
        out_specs=(P("section", "dp", None), P("section", "dp", None)),
        check_vma=False,
    )
```

```python
import math

import jax
import jax.numpy as jnp
from jax import lax
from jax.experimental import pallas as pl
from jax.experimental.pallas import tpu as pltpu
from jax.sharding import PartitionSpec as P

MESH = pl.DeviceIdType.MESH
BF, F32 = jnp.bfloat16, jnp.float32
C, H, T = 640, 2560, 64
ROWS, LANES = 80, 128
PLANS = 5
BLOCKS = 128
HALF = H // 2
STREAMS = (slice(0, 48), slice(48, 80))
COLS = (slice(0, 256), slice(256, C))
UNITS = [(h, p) for h in range(2) for p in range(PLANS)]

_FOUR, _ONE = ["xu", "yu", "za", "xv", "yv"], ["yu", "za", "yv"]
_TURN = [[0, 0], [1, 1], [2, 2], [0, 2], [1, 2]]
FOUR = [[["zb"] + [_FOUR[(p + i) % 5] for i in range(5)] for h in range(2)] for p in range(PLANS)]
ONE = [[["zb"] + [_ONE[(_TURN[p][h] + i) % 3] for i in range(3)] for h in range(2)] for p in range(PLANS)]


def place(order, s, zl, y, c):
    xu, yu = lax.div(s, 2), lax.div(y, 2)
    bits = {
        "xu": xu, "xv": lax.rem(lax.rem(s, 2) + xu, 2),
        "yu": yu, "yv": lax.rem(lax.rem(y, 2) + yu, 2),
        "za": lax.rem(zl, 2), "zb": lax.div(zl, 2),
    }
    at = c * (1 << len(order))
    for i, name in enumerate(order):
        at = at + bits[name] * (1 << i)
    return at


def kernel(b_ref, w_ref, gain_ref, cot_ref, wg_ref, sg_ref,
           g, r, w, wt, gains, xh, dn, acts, acts_o, dpre, dpre_o, cs, cs_o, gs, gs_o,
           c_in, c_out, g_out, x_send, x_back,
           ag_s, ag_r, co_s, co_r, rs_s, rs_r, gn_s, gn_r, hop_s, sg_s, sg_r, ex_s, ex_r,
           up_s, up_r, down_s, down_r, relay_s, relay_r):
    sec, dp = lax.axis_index("section"), lax.axis_index("dp")
    j, x = lax.div(sec, 4), lax.rem(sec, 4)
    zl, y, c = lax.div(dp, 8), lax.rem(lax.div(dp, 2), 4), lax.rem(dp, 2)

    def device(j, x, zl, y, c):
        return (j * 4 + x, zl * 8 + y * 2 + c)

    def flip(v):
        return v + 1 - 2 * lax.rem(v, 2)

    partner = {
        "xu": device(j, 3 - x, zl, y, c),
        "xv": device(j, flip(x), zl, y, c),
        "yu": device(j, x, zl, 3 - y, c),
        "yv": device(j, x, zl, flip(y), c),
        "za": device(j, x, flip(zl), y, c),
        "zb": device(j, x, lax.rem(zl + 2, 4), y, c),
    }
    core_partner = device(j, x, zl, y, 1 - c)
    ahead = device(lax.rem(j + 1, 4), x, zl, y, c)
    behind = device(lax.rem(j + 3, 4), x, zl, y, c)
    beside = [device(j, lax.rem(x + i, 4), zl, y, c) for i in (1, 2, 3)]

    barrier = pltpu.get_barrier_semaphore()
    peers = list(partner.values()) + [core_partner, beside[1]]

    def greet(peer):
        pl.semaphore_signal(barrier, inc=1, device_id=peer, device_id_type=MESH)

    for peer in peers:
        greet(peer)

    def own_shard(orders, s):
        for h, p in UNITS:
            g[p, place(orders[p][h], s, zl, y, c), STREAMS[h]] = w_ref[0, STREAMS[h], p * LANES:(p + 1) * LANES]
        gains[s] = jnp.concatenate(
            [gain_ref[:, (2 * i + h) * ROWS:(2 * i + h + 1) * ROWS] for h in (0, 1) for i in range(16)], axis=1
        )

    last = device(0, 3, zl, y, c)

    @pl.when(j == 0)
    def _():
        own_shard(ONE, 0)
        pl.semaphore_wait(barrier, len(peers))

        @pl.when(x == 3)
        def _():
            for m in range(3):
                greet(device(1, m, zl, y, c))

    @pl.when(j > 0)
    def _():
        own_shard(FOUR, x)

        @pl.when((j == 1) & (x < 3))
        def _():
            pl.semaphore_wait(barrier, len(peers) + 2)

        @pl.when((j > 1) | (x == 3))
        def _():
            pl.semaphore_wait(barrier, len(peers) + 1)

        greet(behind)

    @pl.when(j < 3)
    def _():
        greet(ahead)

    def remote(src, dst, send, recv, to):
        return pltpu.make_async_remote_copy(
            src_ref=src, dst_ref=dst, send_sem=send, recv_sem=recv, device_id=to, device_id_type=MESH
        )

    def held(at, step):
        n = 1 << step
        return lax.div(at, n) * n

    def other(at, step):
        n = 1 << step
        return held(at, step) + n - 2 * n * lax.rem(lax.div(at, n), 2)

    def gathering(orders, s):
        steps = len(orders[0][0])

        def own(h, p):
            return place(orders[p][h], s, zl, y, c)

        def gather(h, p, step, late):
            if step:
                first, n = (other if late else held)(own(h, p), step - 1), 1 << (step - 1)
            else:
                first, n = own(h, p), 1
            part = g.at[p, pl.ds(first, n), STREAMS[h]]
            return remote(part, part, ag_s.at[step, late, p, h], ag_r.at[step, late, p, h], partner[orders[p][h][step]])

        def arrive(h, p, step):
            if step:
                gather(h, p, step, 0).wait_recv()
            gather(h, p, step, 1).wait_recv()

        def across(h, p, late):
            first = (other if late else held)(own(h, p), steps - 1)
            part = g.at[p, pl.ds(first, 1 << (steps - 1)), STREAMS[h]]
            return remote(part, part, co_s.at[late, p, h], co_r.at[late, p, h], core_partner)

        for unit in UNITS:
            gather(*unit, 0, 1).start()
        for unit in UNITS:
            gather(*unit, 1, 0).start()
        for step in range(1, steps):
            for unit in UNITS:
                arrive(*unit, step - 1)
                gather(*unit, step, 1).start()
                if step + 1 < steps:
                    gather(*unit, step + 1, 0).start()
                else:
                    across(*unit, 0).start()
        for unit in UNITS:
            arrive(*unit, steps - 1)
            across(*unit, 1).start()
        for unit in UNITS:
            across(*unit, 0).wait_recv()
            across(*unit, 1).wait_recv()

        def sends_done():
            for unit in UNITS:
                for step in range(steps):
                    if step:
                        gather(*unit, step, 0).wait_send()
                    gather(*unit, step, 1).wait_send()
                across(*unit, 0).wait_send()
                across(*unit, 1).wait_send()

        return sends_done

    gain_copies = [
        remote(gains.at[x], gains.at[x], gn_s.at[i], gn_r.at[i], beside[i]) for i in range(3)
    ]

    def repack_four(i, carry):
        s, k = lax.div(i, 32), lax.rem(i, 32)
        c_, z_, y_ = lax.div(k, 16), lax.rem(lax.div(k, 4), 4), lax.rem(k, 4)
        for p in range(PLANS):
            at = place(FOUR[p][0], s, z_, y_, c_)
            w[s, pl.ds(pl.multiple_of(k * ROWS, 16), ROWS), p * LANES:(p + 1) * LANES] = g[p, at]
        return carry

    def repack_one(k, carry):
        c_, z_, y_ = lax.div(k, 16), lax.rem(lax.div(k, 4), 4), lax.rem(k, 4)
        for h, p in UNITS:
            rows = STREAMS[h]
            at = place(ONE[p][h], x, z_, y_, c_)
            to = pl.ds(pl.multiple_of(k * ROWS + rows.start, 16), rows.stop - rows.start)
            w[0, to, p * LANES:(p + 1) * LANES] = g[p, at, rows]
        return carry

    def transpose(i, carry):
        s, k = lax.div(i, 10), lax.rem(i, 10)
        at = pl.ds(pl.multiple_of(k * 256, 256), 256)
        wt[s, :, at] = w[s, at, :].T
        return carry

    def hop(src, dst, sems, i, part, to):
        cols = COLS[part]
        return remote(src.at[:, cols], dst.at[:, cols], sems[0].at[i, part], sems[1].at[i, part], to)

    UP, DOWN = (up_s, up_r), (down_s, down_r)

    def fwd(part, src):
        return hop(src, cs.at[0], (hop_s, up_r), 0, part, ahead)

    def bwd(part):
        return hop(g_out, gs.at[3], (hop_s, down_r), 1, part, behind)

    def bwd_last(part):
        cols = COLS[part]
        return remote(g_out.at[:, cols], gs.at[x, :, cols], hop_s.at[1, part], down_r.at[x, part], last)

    def up(m, part):
        return hop(x_send.at[m], cs.at[m], UP, m, part, device(j, lax.rem(x + 1, 4), zl, y, c))

    def down(m, part):
        return hop(x_back.at[m], gs.at[m], DOWN, m, part, device(j, lax.rem(x + 3, 4), zl, y, c))

    def relay(m, part):
        cols = COLS[part]
        return remote(x_send.at[m, :, cols], c_in.at[:, cols], relay_s.at[m, part], relay_r.at[0, part], device(j, m, zl, y, c))

    def by_parts(value, weight, arrived):
        if arrived is None:
            return jnp.dot(value[...], weight[...], preferred_element_type=F32)
        arrived(0)
        total = jnp.dot(value[:, COLS[0]], weight[COLS[0], :], preferred_element_type=F32)
        arrived(1)
        return total + jnp.dot(value[:, COLS[1]], weight[COLS[1], :], preferred_element_type=F32)

    def leave(block, change, s, send):
        for part, cols in enumerate(COLS):
            out = block[:, cols].astype(F32) + jnp.dot(change, w[s, :, cols], preferred_element_type=F32)
            send(part, out.astype(BF))

    def forward(i, s, send, arrived=None, ready=True):
        if ready:
            pre = by_parts(cs.at[i], wt.at[s], arrived)
        else:
            if arrived is not None:
                arrived(0)
                arrived(1)
            pre = lax.dot_general(cs[i], w[s], (((1,), (1,)), ((), ())), preferred_element_type=F32)
        inv = lax.rsqrt(jnp.mean(pre * pre, axis=1, keepdims=True) + 1e-05)
        hat = pre * inv
        gain = gains[s]
        normed = hat * gain
        sig = 1.0 / (1.0 + jnp.exp(-normed))
        act = (normed * sig).astype(BF)
        leave(cs.at[i], act, s, send)
        xh[i] = hat
        dn[i] = sig * (1.0 + normed * (1.0 - sig)) * gain * inv
        acts[i, 0] = act[:, :HALF]
        acts[i, 1] = act[:, HALF:]

    @pl.when(j == 0)
    def _():
        sends_done = gathering(ONE, x)
        lax.fori_loop(0, 32, repack_one, 0)
        lax.fori_loop(0, 10, transpose, 0)

        @pl.when(x == 0)
        def _():
            for m in range(4):
                cs[m] = b_ref[m * T:(m + 1) * T, :]

        def step(m, carry):
            def arrived(part):
                @pl.when(x > 0)
                def _():
                    up(m, part).wait_recv()

            def send(part, value):
                x_send[m, :, COLS[part]] = value

                @pl.when(x < 3)
                def _():
                    up(m, part).start()

                @pl.when((x == 3) & (m < 3))
                def _():
                    relay(m, part).start()

            forward(m, 0, send, arrived)
            return carry

        lax.fori_loop(0, 4, step, 0)
        pl.semaphore_wait(barrier, 1)
        for part in range(2):
            @pl.when(x == 3)
            def _():
                fwd(part, x_send.at[3]).start()

            @pl.when(x < 3)
            def _():
                relay(0, part).wait_recv()
                fwd(part, c_in).start()

        sends_done()

    @pl.when(j > 0)
    def _():
        for copy in gain_copies:
            copy.start()
        sends_done = gathering(FOUR, x)
        for copy in gain_copies:
            copy.wait()
        lax.fori_loop(0, 4 * 32, repack_four, 0)

        def arrived(part):
            fwd(part, c_out).wait_recv()

        def stage(ready):
            def within(s, carry):
                def send(part, value):
                    cs[s + 1, :, COLS[part]] = value

                forward(s, s, send, ready=ready)
                return carry

            def send(part, value):
                c_out[:, COLS[part]] = value
                fwd(part, c_out).start()

            def end(part, value):
                pass

            def first(part, value):
                cs[1, :, COLS[part]] = value

            forward(0, 0, first, arrived, ready)
            lax.fori_loop(1, 3, within, 0)

            @pl.when(j < 3)
            def _():
                pl.semaphore_wait(barrier, 1)
                forward(3, 3, send, ready=ready)

            if ready:
                @pl.when(j == 3)
                def _():
                    forward(3, 3, end)

        @pl.when(j == 1)
        def _():
            stage(False)
            lax.fori_loop(0, 40, transpose, 0)

        @pl.when(j > 1)
        def _():
            lax.fori_loop(0, 40, transpose, 0)
            stage(True)

        sends_done()

    ex = [
        remote(acts.at[:, 1 - c], acts_o, ex_s.at[0], ex_r.at[0], core_partner),
        remote(cs, cs_o, ex_s.at[1], ex_r.at[1], core_partner),
    ]

    @pl.when(j < 3)
    def _():
        ex[0].start()
        ex[1].start()

    def ex_dpre(s):
        return remote(dpre.at[s, 1 - c], dpre_o.at[s], ex_s.at[2 + s], ex_r.at[2 + s], core_partner)

    def ex_grad(s):
        return remote(gs.at[s], gs_o.at[s], ex_s.at[6 + s], ex_r.at[6 + s], core_partner)

    def backward(i, s, send, arrived=None):
        e = by_parts(gs.at[i], wt.at[s], arrived) * dn[i]
        hat = xh[i]
        dp = (e - hat * jnp.mean(e * hat, axis=1, keepdims=True)).astype(BF)
        leave(gs.at[i], dp, s, send)
        dpre[i, 0] = dp[:, :HALF]
        dpre[i, 1] = dp[:, HALF:]
        ex_grad(i).start()
        ex_dpre(i).start()

    rows = pl.ds(pl.multiple_of(x * T, T), T)
    sg_copies = [
        remote(x_back.at[lax.rem(x + i, 4)], sg_ref.at[0, rows], sg_s.at[i - 1], sg_r.at[i - 1], beside[i - 1])
        for i in (1, 2, 3)
    ]

    @pl.when(j == 0)
    def _():
        def step(m, carry):
            def arrived(part):
                down(m, part).wait_recv()

            def send(part, value):
                x_back[m, :, COLS[part]] = value

                @pl.when(x > 0)
                def _():
                    down(m, part).start()

            backward(m, 0, send, arrived)
            sg_ref[0, pl.ds(pl.multiple_of(m * T, T), T), :] = x_back[m]
            return carry

        lax.fori_loop(0, 4, step, 0)

    @pl.when(j > 0)
    def _():
        @pl.when(j == 3)
        def _():
            gs[3] = cot_ref[rows, :]

        def arrived(part):
            @pl.when(j < 3)
            def _():
                bwd(part).wait_recv()

        def first(part, value):
            gs[2, :, COLS[part]] = value
            x_back[3, :, COLS[part]] = value

        def step(i, carry):
            s = 3 - i

            def send(part, value):
                gs[s - 1, :, COLS[part]] = value
                x_back[s, :, COLS[part]] = value

            backward(s, s, send)
            return carry

        def out(part, value):
            g_out[:, COLS[part]] = value

            @pl.when(j == 1)
            def _():
                bwd_last(part).start()

            @pl.when(j > 1)
            def _():
                bwd(part).start()

            x_back[0, :, COLS[part]] = value

        backward(3, 3, first, arrived)
        lax.fori_loop(1, 3, step, 0)
        backward(0, 0, out)
        sg_ref[0, rows, :] = x_back[x]
        for copy in sg_copies:
            copy.start()

    @pl.when(j == 3)
    def _():
        ex[0].start()
        ex[1].start()

    ex[0].wait_recv()
    ex[1].wait_recv()

    def left_of(i, at):
        return [dpre[i, c, :, at], dpre_o[i, :, at], acts[i, c, :, at], acts_o[i, :, at]]

    def right_of(i):
        return [cs[i], cs_o[i], gs[i], gs_o[i]]

    def outer(left, right):
        left, right = jnp.concatenate(left, axis=0), jnp.concatenate(right, axis=0)
        return lax.dot_general(left, right, (((0,), (0,)), ((), ())), preferred_element_type=F32).astype(BF)

    def summing(orders, s):
        steps = len(orders[0][0])

        def own(h, p):
            return place(orders[p][h], s, zl, y, 0)

        def reduce(h, p, step):
            n = 1 << step
            return remote(
                g.at[p, pl.ds(other(own(h, p), step), n), STREAMS[h]],
                r.at[p, pl.ds(n - 1, n), STREAMS[h]],
                rs_s.at[step, p, h], rs_r.at[step, p, h], partner[orders[p][h][step]],
            )

        for unit in UNITS:
            reduce(*unit, steps - 1).start()
        for step in range(steps - 1, -1, -1):
            for h, p in UNITS:
                n = 1 << step
                base = held(own(h, p), step)
                reduce(h, p, step).wait_recv()

                def add(start, count, p=p, h=h, n=n, base=base):
                    def one(i, carry):
                        at = start + i
                        g[p, at, STREAMS[h]] = g[p, at, STREAMS[h]] + r[p, n - 1 + at - base, STREAMS[h]]
                        return carry

                    lax.fori_loop(0, count, one, 0, unroll=min(count, 8))

                if step:
                    add(other(own(h, p), step - 1), n // 2)
                    reduce(h, p, step - 1).start()
                    add(held(own(h, p), step - 1), n // 2)
                else:
                    add(base, 1)

        for h, p in UNITS:
            total = g[p, own(h, p), STREAMS[h]].astype(F32)
            wg_ref[0, STREAMS[h], p * LANES:(p + 1) * LANES] = total * (1.0 / math.sqrt(8192))
        for unit in UNITS:
            for step in range(steps):
                reduce(*unit, step).wait_send()

    @pl.when(j == 0)
    def _():
        right = []
        for m in range(4):
            ex_grad(m).wait_recv()
            ex_dpre(m).wait_recv()
            right += right_of(m)
        for zh in range(2):
            at = slice(zh * 640, zh * 640 + 640)
            grad = outer([v for m in range(4) for v in left_of(m, at)], right)
            for t in range(8):
                for h, p in UNITS:
                    rows = STREAMS[h]
                    to = place(ONE[p][h], x, 2 * zh + t // 4, t % 4, 0)
                    g[p, to, rows] = grad[t * ROWS + rows.start:t * ROWS + rows.stop, p * LANES:(p + 1) * LANES]
        summing(ONE, x)

    @pl.when(j > 0)
    def _():
        def section(i, carry):
            s = 3 - i
            ex_grad(s).wait_recv()
            ex_dpre(s).wait_recv()
            for zh in range(2):
                grad = outer(left_of(s, slice(zh * 640, zh * 640 + 640)), right_of(s))
                for t in range(8):
                    for p in range(PLANS):
                        to = place(FOUR[p][0], s, 2 * zh + t // 4, t % 4, 0)
                        g[p, to] = grad[t * ROWS:(t + 1) * ROWS, p * LANES:(p + 1) * LANES]
            return carry

        lax.fori_loop(0, 4, section, 0)
        summing(FOUR, x)
        for copy in sg_copies:
            copy.wait()

    ex[0].wait_send()
    ex[1].wait_send()

    def sent(s, carry):
        ex_grad(s).wait_send()
        ex_dpre(s).wait_send()
        return carry

    lax.fori_loop(0, 4, sent, 0)

    for part in range(2):
        @pl.when(j < 3)
        def _():
            fwd(part, c_out).wait_send()

        @pl.when(j > 0)
        def _():
            bwd(part).wait_send()

    @pl.when(j == 0)
    def _():
        def sent(m, carry):
            for part in range(2):
                @pl.when(x < 3)
                def _():
                    up(m, part).wait_send()

                @pl.when((x == 3) & (m < 3))
                def _():
                    relay(m, part).wait_send()

                @pl.when(x > 0)
                def _():
                    down(m, part).wait_send()

            return carry

        lax.fori_loop(0, 4, sent, 0)


def shards(boundary_in, weights, gains, cotangent):
    vmem = pl.BlockSpec(memory_space=pltpu.VMEM)
    dma = pltpu.SemaphoreType.DMA
    return pl.pallas_call(
        kernel,
        out_shape=(
            jax.ShapeDtypeStruct((1, ROWS, C), F32),
            jax.ShapeDtypeStruct((1, 4 * T, C), BF),
        ),
        in_specs=[vmem] * 4,
        out_specs=(vmem, vmem),
        scratch_shapes=[
            pltpu.VMEM((PLANS, BLOCKS, ROWS, LANES), BF),
            pltpu.VMEM((PLANS, BLOCKS // 2 - 1, ROWS, LANES), BF),
            pltpu.VMEM((4, H, C), BF),
            pltpu.VMEM((4, C, H), BF),
            pltpu.VMEM((4, 1, H), F32),
            pltpu.VMEM((4, T, H), F32),
            pltpu.VMEM((4, T, H), F32),
            pltpu.VMEM((4, 2, T, HALF), BF),
            pltpu.VMEM((4, T, HALF), BF),
            pltpu.VMEM((4, 2, T, HALF), BF),
            pltpu.VMEM((4, T, HALF), BF),
            pltpu.VMEM((4, T, C), BF),
            pltpu.VMEM((4, T, C), BF),
            pltpu.VMEM((4, T, C), BF),
            pltpu.VMEM((4, T, C), BF),
            pltpu.VMEM((T, C), BF),
            pltpu.VMEM((T, C), BF),
            pltpu.VMEM((T, C), BF),
            pltpu.VMEM((4, T, C), BF),
            pltpu.VMEM((4, T, C), BF),
            dma((6, 2, PLANS, 2)),
            dma((6, 2, PLANS, 2)),
            dma((2, PLANS, 2)),
            dma((2, PLANS, 2)),
            dma((6, PLANS, 2)),
            dma((6, PLANS, 2)),
            dma((3,)),
            dma((3,)),
            dma((2, 2)),
            dma((3,)),
            dma((3,)),
            dma((10,)),
            dma((10,)),
            dma((4, 2)),
            dma((4, 2)),
            dma((4, 2)),
            dma((4, 2)),
            dma((3, 2)),
            dma((1, 2)),
        ],
        compiler_params=pltpu.CompilerParams(
            collective_id=0, has_side_effects=True, vmem_limit_bytes=60 << 20
        ),
    )(boundary_in, weights, gains, cotangent)


def solution(mesh):
    return jax.shard_map(
        shards,
        mesh=mesh,
        in_specs=(P("dp", None), P("section", "dp", None), P("section", None), P("dp", None)),
        out_specs=(P("section", "dp", None), P("section", "dp", None)),
        check_vma=False,
    )
```
